256 devices in a mesh: dp: 8 (over y, core), expert: 32 (over x, z).
Axes of the slice: x: 4, y: 4, z: 8, core: 2. Of those that a mesh axis runs over, the one named last changes fastest.
Arguments:
- tokens: bfloat16 [2048, 7168], P(('dp', 'expert')), may hold values from -6 to 6
- routes: int32 [2048, 8], P(('dp', 'expert')), may hold values from 0 to 31, all different within a row; in each aligned block of 8 rows (0 to 7, 8 to 15, ...) at most 4 rows name the same one
- group_of: int32 [32], replicated, may hold values from 0 to 7, as said below
- sketch_map: bfloat16 [7168, 64], P('dp'), may hold values from -0.0625 to 0.0625
- gate_weight: bfloat16 [32, 7168, 2048], P('expert', None, 'dp'), may hold values from -0.0625 to 0.0625
- up_weight: bfloat16 [32, 7168, 2048], P('expert', None, 'dp'), may hold values from -0.0625 to 0.0625
- down_weight: bfloat16 [32, 2048, 7168], P('expert', 'dp'), may hold values from -0.125 to 0.125
Outputs:
- cross_moment: float32 [8, 64, 7168], P(None, None, 'dp')
- gram_moment: float32 [8, 64, 64], replicated
- output_sum: float32 [8, 7168], P(None, 'dp')
The draws below stay inside these ranges and needn't reach their ends.
Inputs may be any that keep to these rules, and one draw needn't show every extreme that they name: `routes`: each row names 8 different experts. Among the 8 rows of one device no expert is named more than 4 times, a bound that some block reaches. `group_of`: every merge group has at least one expert.
All inputs are finite; a program needn't handle non-finite values.
Results may differ from the reference program's by a relative error of at most 0.0065.
Values may be sent and summed in bfloat16 or wider, within the bound.
No kernel may reach another device: no remote copies, remote signals or barrier semaphores. Data moves between devices by JAX's collectives and lax.ppermute only.
A program may use at most 128 MiB of HBM per device.

```python
import math
import jax
import jax.numpy as jnp
import numpy as np
from jax import lax

D = 7168
FF = 2048
SKETCH = 64
TOPK = 8
EXPERTS = 32
GROUPS = 8
TOK_DEV = 8
CAP = 4
ROWS = 1024
TOKENS = 2048


def draw_group_of(key, part):
    key = jax.random.fold_in(key, 11)
    first_key, second_key = jax.random.split(key)
    shuffled = jax.random.permutation(first_key, EXPERTS)
    spare_ids = jax.random.randint(second_key, (EXPERTS,), 0, GROUPS)
    return jnp.where(shuffled < GROUPS, shuffled, spare_ids).astype(jnp.int32)


def levels(rng, dims, shards, least, largest):
    level, own = 1.0, jax.random.fold_in(rng, 6)
    for axis_at, blocks in shards:
        steps = jnp.exp(jax.random.uniform(jax.random.fold_in(own, axis_at), (blocks,), jnp.float32, least / len(shards), largest / len(shards)))
        level = level * jnp.repeat(steps, dims[axis_at] // blocks).reshape([-1 if axis == axis_at else 1 for axis in range(len(dims))])
    return level


def shared_out(stream_key, own, number, rows, amount, top, reach, lean):
    sequence = jax.random.permutation(stream_key, amount)
    crowded, ordinary = portions_of(amount, rows * top, reach, lean, True), portions_of(amount, rows * top, reach, lean, False)
    places = jnp.arange(amount)

    def named(sizes, offset_by):
        used = int((sizes > 0).sum())
        fixed = max(1, used // 4)
        passed = fixed + (places - fixed + offset_by * (used - fixed)) % max(1, amount - fixed)
        return jnp.zeros((amount,), jnp.int32).at[sequence[jnp.where(places < fixed, places, passed)]].set(jnp.asarray(sizes, jnp.int32))

    sizes = jnp.where(number % 4 == 0, named(crowded, number // 4), named(ordinary, number - number // 4 - 1))
    mixed = jax.random.permutation(jax.random.fold_in(own, 3), amount)
    donor, taker = mixed[0:amount // 2 * 2:2], mixed[1:amount // 2 * 2:2]
    slack = jnp.minimum(sizes[donor] - 1, reach - sizes[taker]) // 2
    slack = jnp.where((donor == sequence[0]) | (taker == sequence[0]) | (sizes[taker] == 0), 0, jnp.maximum(slack, 0))
    passed = jax.random.randint(jax.random.fold_in(own, 4), (amount // 2,), 0, 1 << 20) % (slack + 1)
    sizes = sizes.at[donor].add(-passed).at[taker].add(passed)
    members = jnp.searchsorted(jnp.cumsum(sizes), jnp.arange(rows * top), side="right").astype(jnp.int32)
    grid = members.reshape(top, rows).T
    grid = grid[jax.random.permutation(jax.random.fold_in(own, 1), rows)]
    offset_by = jax.random.randint(jax.random.fold_in(own, 2), (rows, 1), 0, top)
    return jnp.take_along_axis(grid, (jnp.arange(top)[None, :] + offset_by) % top, axis=1)


def portions_of(number_of, total, reach, skew, full):
    loads = [(1 << 20) // math.isqrt(standing ** skew) + 1 for standing in range(1, number_of + 1)]
    largest = reach if full else min(reach, max(-(-total // number_of), total * loads[0] // sum(loads)))
    least = 1 if total - largest >= number_of - 1 else 0
    given, rest = [largest] + [least] * (number_of - 1), total - largest - least * (number_of - 1)
    while rest > 0:
        candidates = [i for i in range(1, number_of) if given[i] < largest] or [i for i in range(1, number_of) if given[i] < reach]
        whole, budget = sum([loads[i] for i in candidates]), rest
        for i in candidates:
            more = min(reach - given[i], max(1, budget * loads[i] // whole), rest)
            given[i] = given[i] + more
            rest = rest - more
    return np.array(given)


def normal_values(rng, dims, width, limit, cuts=(), held_as=jnp.bfloat16):
    result = jax.random.normal(rng, dims, jnp.float32) * width
    if len(cuts) > 0:
        result = levels(rng, dims, cuts, -0.22, 0.18) * result
    return jnp.clip(result, min=-limit, max=limit).astype(held_as)


def setup_inputs(seed: int = 0) -> dict:
    keys = jax.random.split(jax.random.key(seed), 8)
    tokens = normal_values(keys[0], (TOKENS, D), 1.0, 6.0, ((0, 256),))
    routes_keys = jax.random.split(jax.random.fold_in(keys[1], 1), TOKENS // TOK_DEV)
    routes_turns = jax.random.permutation(jax.random.fold_in(keys[1], 3), TOKENS // TOK_DEV)
    routes = jax.vmap(lambda own, number: shared_out(jax.random.fold_in(keys[1], 2), own, number, TOK_DEV, EXPERTS, TOPK, CAP, 2))(routes_keys, routes_turns).reshape((TOKENS, TOPK))
    group_of = draw_group_of(jax.random.fold_in(keys[7], 71), 0)
    sketch_map = normal_values(keys[3], (D, SKETCH), D ** -0.5, 0.0625, ((0, 8),))
    gate_weight = normal_values(keys[4], (EXPERTS, D, FF), D ** -0.5, 0.0625, ((0, 32), (2, 8)))
    up_weight = normal_values(keys[5], (EXPERTS, D, FF), D ** -0.5, 0.0625, ((0, 32), (2, 8)))
    down_weight = normal_values(keys[6], (EXPERTS, FF, D), FF ** -0.5, 0.125, ((0, 32), (1, 8)))
    return {"tokens": tokens, "routes": routes, "group_of": group_of, "sketch_map": sketch_map, "gate_weight": gate_weight, "up_weight": up_weight, "down_weight": down_weight}


def reference(tokens, routes, group_of, sketch_map, gate_weight, up_weight, down_weight):
    sketch = jnp.dot(tokens, sketch_map, preferred_element_type=jnp.float32).astype(jnp.bfloat16)
    position = jnp.arange(TOKENS, dtype=jnp.int32)
    zero_half = jnp.zeros((), jnp.bfloat16)

    def per_expert(expert):
        chosen = jnp.any(routes == expert, axis=1)
        sort_keys = jnp.where(chosen, position, position + TOKENS)
        picked = jnp.argsort(sort_keys)[:ROWS].astype(jnp.int32)
        present = chosen[picked][:, None]
        chosen_rows = jnp.where(present, tokens[picked], zero_half)
        chosen_sketch = jnp.where(present, sketch[picked], zero_half).astype(jnp.float32)
        gate_rows = jnp.dot(chosen_rows, gate_weight[expert], preferred_element_type=jnp.float32)
        up_rows = jnp.dot(chosen_rows, up_weight[expert], preferred_element_type=jnp.float32)
        hidden = (jax.nn.silu(gate_rows) * up_rows).astype(jnp.bfloat16)
        outputs = jnp.dot(hidden, down_weight[expert], preferred_element_type=jnp.float32)
        cross_part = jnp.dot(chosen_sketch.T, outputs, precision=lax.Precision.HIGHEST)
        gram_part = jnp.dot(chosen_sketch.T, chosen_sketch, precision=lax.Precision.HIGHEST)
        totals = jnp.sum(outputs, axis=0)
        return cross_part, gram_part, totals

    cross_all, gram_all, total_all = lax.map(per_expert, jnp.arange(EXPERTS, dtype=jnp.int32))
    member = (group_of[None, :] == jnp.arange(GROUPS, dtype=jnp.int32)[:, None]).astype(jnp.float32)
    factor = ROWS ** -0.5
    cross_moment = jnp.einsum("ge,erd->grd", member, cross_all, precision=lax.Precision.HIGHEST) * factor
    gram_moment = jnp.einsum("ge,erk->grk", member, gram_all, precision=lax.Precision.HIGHEST) * (factor * factor)
    output_sum = jnp.einsum("ge,ed->gd", member, total_all, precision=lax.Precision.HIGHEST) * factor
    return cross_moment, gram_moment, output_sum
```

```python
import functools
import math

import jax
import jax.numpy as jnp
from jax import lax
from jax.experimental import pallas as pl
from jax.experimental.pallas import tpu as pltpu
from jax.sharding import Mesh
from jax.sharding import PartitionSpec as P

EXPERTS = 32
GROUPS = 8
SKETCH = 64
LANES = 128
ROWS_OUT = 72


def moments_kernel(steps, expert_ref, x_ref, g0_ref, g1_ref, u0_ref, u1_ref, m_ref, tag_ref, out_ref, acc_g, acc_u, acc_s):
    step = pl.program_id(0)
    x = x_ref[...]
    gate = [jnp.dot(x, r[...], preferred_element_type=jnp.float32) for r in (g0_ref, g1_ref)]
    up = [jnp.dot(x, r[...], preferred_element_type=jnp.float32) for r in (u0_ref, u1_ref)]
    part = jnp.dot(x, m_ref[...], preferred_element_type=jnp.float32)

    @pl.when(step == 0)
    def _():
        for i in range(2):
            acc_g[i] = gate[i]
            acc_u[i] = up[i]
        acc_s[...] = part

    @pl.when(step > 0)
    def _():
        for i in range(2):
            acc_g[i] += gate[i]
            acc_u[i] += up[i]
        acc_s[...] += part

    @pl.when(step == steps - 1)
    def _():
        tag = tag_ref[...].astype(jnp.float32)
        lane = lax.broadcasted_iota(jnp.int32, tag.shape, 1)
        mask = jnp.sum(jnp.where(lane == expert_ref[0], tag, 0.0), axis=1, keepdims=True)
        sketch = acc_s[...].astype(jnp.bfloat16)
        wide = sketch.astype(jnp.float32)
        zeros = jnp.zeros((wide.shape[0], ROWS_OUT - SKETCH - 1), jnp.float32)
        left = jnp.concatenate([wide * mask, mask, zeros], axis=1).astype(jnp.bfloat16)
        contract = (((0,), (0,)), ((), ()))
        for i in range(2):
            gated = acc_g[i]
            hidden = (gated / (1.0 + jnp.exp(-gated)) * acc_u[i]).astype(jnp.bfloat16)
            width = hidden.shape[1]
            out_ref[:ROWS_OUT, i * width : (i + 1) * width] = lax.dot_general(
                left, hidden, contract, preferred_element_type=jnp.float32
            )
        for g in range(GROUPS):
            count = jnp.sum(jnp.where(lane == EXPERTS + g, tag, 0.0), axis=1, keepdims=True)
            scaled = wide * count
            high = scaled.astype(jnp.bfloat16)
            low = (scaled - high.astype(jnp.float32)).astype(jnp.bfloat16)
            both = lax.dot_general(sketch, high, contract, preferred_element_type=jnp.float32)
            both += lax.dot_general(sketch, low, contract, preferred_element_type=jnp.float32)
            out_ref[ROWS_OUT:, g * SKETCH : (g + 1) * SKETCH] = both


def local_moments(expert, ext, gates, ups, sketch_map):
    rows = ext.shape[0]
    width, ff = sketch_map.shape[0], gates[0].shape[1]
    depth = 1024
    steps = width // depth
    weight = pl.BlockSpec((depth, ff), lambda k, e: (k, 0))
    return pl.pallas_call(
        functools.partial(moments_kernel, steps),
        grid_spec=pltpu.PrefetchScalarGridSpec(
            num_scalar_prefetch=1,
            grid=(steps,),
            in_specs=[
                pl.BlockSpec((rows, depth), lambda k, e: (0, k)),
                weight,
                weight,
                weight,
                weight,
                pl.BlockSpec((depth, SKETCH), lambda k, e: (k, 0)),
                pl.BlockSpec((rows, LANES), lambda k, e: (0, width // LANES)),
            ],
            out_specs=pl.BlockSpec((ROWS_OUT + SKETCH, 2 * ff), lambda k, e: (0, 0)),
            scratch_shapes=[
                pltpu.VMEM((2, rows, ff), jnp.float32),
                pltpu.VMEM((2, rows, ff), jnp.float32),
                pltpu.VMEM((rows, SKETCH), jnp.float32),
            ],
        ),
        out_shape=jax.ShapeDtypeStruct((ROWS_OUT + SKETCH, 2 * ff), jnp.float32),
        compiler_params=pltpu.CompilerParams(vmem_limit_bytes=48 * 2**20),
        name="local_moments",
    )(expert, ext, *gates, *ups, sketch_map, ext)


def down_kernel(own_ref, other_ref, w0_ref, w1_ref, out_ref):
    width = w0_ref.shape[0]
    total = None
    for left, weight in (
        (own_ref[:, :width] + other_ref[:, width:], w0_ref),
        (own_ref[:, width:] + other_ref[:, :width], w1_ref),
    ):
        high = left.astype(jnp.bfloat16)
        low = (left - high.astype(jnp.float32)).astype(jnp.bfloat16)
        both = jnp.dot(high, weight[...], preferred_element_type=jnp.float32)
        both += jnp.dot(low, weight[...], preferred_element_type=jnp.float32)
        total = both if total is None else total + both
    for t in range(out_ref.shape[1]):
        out_ref[0, t] = total[:, t * LANES : (t + 1) * LANES].astype(out_ref.dtype)


def down_moments(own, other, own_down, other_down, blocks):
    ff, columns = own_down.shape
    block = columns // blocks
    left = pl.BlockSpec((ROWS_OUT, 2 * ff), lambda j: (0, 0))
    weight = pl.BlockSpec((ff, block), lambda j: (0, j))
    return pl.pallas_call(
        down_kernel,
        grid=(blocks,),
        in_specs=[left, left, weight, weight],
        out_specs=pl.BlockSpec((1, block // LANES, ROWS_OUT, LANES), lambda j: (j, 0, 0, 0)),
        out_shape=jax.ShapeDtypeStruct((blocks, block // LANES, ROWS_OUT, LANES), jnp.bfloat16),
        name="down_moments",
    )(own, other, own_down, other_down)


def shards(tokens, routes, group_of, sketch_map, gate_weight, up_weight, down_weight):
    gate, up, down = gate_weight[0], up_weight[0], down_weight[0]
    swap = functools.partial(lax.ppermute, axis_name="core", perm=[(0, 1), (1, 0)])
    core = lax.axis_index("core")
    n_y, n_xz = lax.axis_size("y"), lax.axis_size("x") * lax.axis_size("z")
    expert = lax.axis_index("x") * lax.axis_size("z") + lax.axis_index("z")

    member = (group_of[:, None] == lax.iota(jnp.int32, GROUPS)[None, :]).astype(jnp.float32)
    named = jnp.any(routes[:, :, None] == lax.iota(jnp.int32, EXPERTS), axis=1).astype(jnp.float32)
    counts = jnp.sum(named[:, :, None] * member[None], axis=1)
    tag = jnp.concatenate([named, counts], axis=1).astype(jnp.bfloat16)
    tag = jnp.pad(tag, ((0, 0), (0, LANES - tag.shape[1])))
    ext = jnp.concatenate([tokens, tag], axis=1)
    ext = lax.all_gather(ext, ("y", "x", "z"), axis=0, tiled=True)
    full_map = lax.all_gather(sketch_map, ("y", "core"), axis=0, tiled=True)
    gates, ups = (gate, swap(gate)), (up, swap(up))
    ff, width = down.shape
    halves = down.reshape(ff, n_y, 2, width // (2 * n_y))
    own_down = lax.dynamic_index_in_dim(halves, core, 2, keepdims=False).reshape(ff, width // 2)
    sent = lax.dynamic_index_in_dim(halves, 1 - core, 2, keepdims=False).reshape(ff, width // 2)
    other_down = swap(sent)

    own = local_moments(expert.reshape(1), ext, gates, ups, full_map)
    other = swap(own)
    rows = n_xz * 4 * 8
    factor = 1.0 / math.sqrt(rows)
    gram = (own[ROWS_OUT:] + other[ROWS_OUT:]) * (factor * factor)
    gram_moment = gram.reshape(SKETCH, GROUPS, SKETCH).transpose(1, 0, 2)

    parts = down_moments(own, other, own_down, other_down, n_y)
    parts = lax.all_to_all(parts, "y", split_axis=0, concat_axis=0, tiled=True)
    block = jnp.sum(parts.astype(jnp.float32), axis=0)
    tiles = block.shape[0]
    block = block.reshape(tiles * ROWS_OUT, LANES)
    share = -(-block.shape[0] // (8 * n_xz)) * 8
    block = jnp.pad(block, ((0, share * n_xz - block.shape[0]), (0, 0)))
    pieces = lax.all_to_all(
        block.reshape(n_xz, share, LANES), ("x", "z"), split_axis=0, concat_axis=0, tiled=True
    )
    summed = jnp.einsum("eg,erl->grl", member, pieces, precision=lax.Precision.HIGHEST) * factor
    summed = summed.astype(jnp.bfloat16)
    spread = jnp.broadcast_to(summed[None], (n_xz, *summed.shape))
    spread = lax.all_to_all(spread, ("x", "z"), split_axis=0, concat_axis=0, tiled=True)
    whole = spread.transpose(1, 0, 2, 3).reshape(GROUPS, n_xz * share, LANES)
    whole = whole[:, : tiles * ROWS_OUT].reshape(GROUPS, tiles, ROWS_OUT, LANES)
    whole = whole.astype(jnp.float32).transpose(0, 2, 1, 3).reshape(GROUPS, ROWS_OUT, tiles * LANES)
    return whole[:, :SKETCH], gram_moment, whole[:, SKETCH]


def solution(mesh):
    fine = Mesh(mesh.devices.reshape(4, 2, 4, 8), ("y", "core", "x", "z"))
    dp, expert = ("y", "core"), ("x", "z")
    placed = (
        P((*dp, *expert), None),
        P((*dp, *expert), None),
        P(),
        P(dp, None),
        P(expert, None, dp),
        P(expert, None, dp),
        P(expert, dp, None),
    )
    return jax.shard_map(
        shards,
        mesh=fine,
        in_specs=placed,
        out_specs=(P(None, None, dp), P(), P(None, dp)),
        check_vma=False,
    )
```

```python
import functools
import itertools
import math

import jax
import jax.numpy as jnp
from jax import lax
from jax.experimental import pallas as pl
from jax.experimental.pallas import tpu as pltpu
from jax.sharding import Mesh
from jax.sharding import PartitionSpec as P

EXPERTS = 32
GROUPS = 8
SKETCH = 64
LANES = 128
ROWS_OUT = 72
DEPTH = 896
MAIN = 6
AXES = ("y", "core", "x", "z")
SIZES = (4, 2, 4, 8)
U, V, Z = ("x", "y"), ("y", "x"), ("z", "z")
FF = 256
WIDE = 4 * FF + LANES
VMEM = 48 * 2**20
CONTRACT = (((0,), (0,)), ((), ()))


def shift(block, ring, places):
    pairs = []
    for at in itertools.product(*(range(n) for n in SIZES)):
        source = list(at)
        axis = AXES.index(ring[at[1]])
        source[axis] = (source[axis] + places) % SIZES[axis]
        number = [0, 0]
        for n, a, b in zip(SIZES, source, at):
            number = [number[0] * n + a, number[1] * n + b]
        pairs.append(tuple(number))
    return lax.ppermute(block, AXES, pairs)


def straight(block, ring, size):
    return jnp.concatenate([block] + [shift(block, ring, k) for k in range(1, size)], axis=0)


def ring_of_four(top, bottom, ring):
    after = (shift(top, ring, 1), shift(bottom, ring, 1))
    before = (shift(top, ring, -1), shift(bottom, ring, -1))
    far = (shift(after[0], ring, 1), shift(before[1], ring, -1))
    return (top, bottom), after, before, far


def ring_of_eight(block, ring):
    half = block.shape[0] // 2
    after, before = [shift(block, ring, 1)], [shift(block, ring, -1)]
    for _ in range(2):
        after.append(shift(after[-1], ring, 1))
        before.append(shift(before[-1], ring, -1))
    far = [shift(after[-1][:half], ring, 1), shift(before[-1][half:], ring, -1)]
    return [block, *after, *far, *before[::-1]]


def tag_kernel(group_ref, routes_ref, tokens_ref, main_ref, rest_ref):
    routes = routes_ref[...]
    group = jnp.zeros(routes.shape, jnp.int32)
    for e in range(EXPERTS):
        group = jnp.where(routes == e, group_ref[e], group)
    lane = lax.broadcasted_iota(jnp.int32, (routes.shape[0], LANES), 1)
    tag = jnp.zeros(lane.shape, jnp.float32)
    for j in range(routes.shape[1]):
        tag += jnp.where(lane == routes[:, j : j + 1], 1.0, 0.0)
        tag += jnp.where(lane == EXPERTS + group[:, j : j + 1], 1.0, 0.0)
    split = rest_ref.shape[1]
    main_ref[:, : MAIN * DEPTH] = tokens_ref[:, : MAIN * DEPTH]
    main_ref[:, MAIN * DEPTH :] = tag.astype(jnp.bfloat16)
    rest_ref[...] = tokens_ref[:, tokens_ref.shape[1] - split :]


def tagged(group_of, routes, tokens):
    rows, width = tokens.shape
    whole = pl.BlockSpec(memory_space=pltpu.VMEM)
    return pl.pallas_call(
        tag_kernel,
        in_specs=[pl.BlockSpec(memory_space=pltpu.SMEM), whole, whole],
        out_specs=[whole, whole],
        out_shape=[
            jax.ShapeDtypeStruct((rows, MAIN * DEPTH + LANES), tokens.dtype),
            jax.ShapeDtypeStruct((rows, width - MAIN * DEPTH), tokens.dtype),
        ],
        name="tag",
    )(group_of, routes, tokens)


def gathered_map(sketch_map, swap):
    half = sketch_map.shape[0] // 2
    own = jnp.concatenate([sketch_map[:half], sketch_map[half:]], axis=1)
    return straight(jnp.stack([own, swap(own)]), ("y", "y"), 4)


def map_block(k, place_ref):
    return lax.rem(k // 2 + 4 - place_ref[1], 4) * 2 + lax.rem(k + place_ref[2], 2), 0, 0


def products(x_refs, w_refs):
    x = jnp.concatenate([r[...] for r in x_refs], axis=0) if len(x_refs) > 1 else x_refs[0][...]
    sides = w_refs[4][0]
    weights = [r[...] for r in w_refs[:4]]
    weights.append(jnp.concatenate([sides[:, :SKETCH], sides[:, SKETCH:]], axis=0))
    return [jnp.dot(x, w, preferred_element_type=jnp.float32) for w in weights]


def weight_specs(weights, first):
    half = weights[4].shape[1]
    return [pl.BlockSpec((DEPTH, w.shape[1]), lambda k, p: (first + k, 0)) for w in weights[:4]] + [
        pl.BlockSpec((1, half, LANES), lambda k, p: map_block(first + k, p))
    ]


def rest_kernel(count, place_ref, *refs):
    x_refs, w_refs, (near_ref, far_ref) = refs[:count], refs[count:-2], refs[-2:]
    step = pl.program_id(0)
    parts = products(x_refs, w_refs)

    def put(ref, at, z, lanes, value):
        @pl.when(step == 0)
        def _():
            ref[at, :, z, :, lanes] = value

        @pl.when(step > 0)
        def _():
            ref[at, :, z, :, lanes] += value

    for i, part in enumerate(parts):
        lanes = slice(i * FF, i * FF + part.shape[1])
        part = part.reshape(8, 4, 4, 8, part.shape[1])
        for z in range(8):
            for at, v in enumerate((0, 1, 3)):
                put(near_ref, at, z, lanes, part[z, v])
            put(far_ref, 0, z, lanes, part[z, 2])


def cost(rows, depth, out_bytes):
    return pl.CostEstimate(
        flops=2 * rows * depth * 5 * FF, bytes_accessed=depth * (rows + WIDE) * 2 + out_bytes, transcendentals=0
    )


def rest_products(place, blocks, weights):
    steps = blocks[0].shape[1] // DEPTH
    shape = (4, 8, 8, WIDE)
    return pl.pallas_call(
        functools.partial(rest_kernel, len(blocks)),
        grid_spec=pltpu.PrefetchScalarGridSpec(
            num_scalar_prefetch=1,
            grid=(steps,),
            in_specs=[pl.BlockSpec((b.shape[0], DEPTH), lambda k, p: (0, k)) for b in blocks]
            + weight_specs(weights, MAIN),
            out_specs=[pl.BlockSpec((n, *shape), lambda k, p: (0, 0, 0, 0, 0)) for n in (3, 1)],
        ),
        out_shape=[jax.ShapeDtypeStruct((n, *shape), jnp.float32) for n in (3, 1)],
        compiler_params=pltpu.CompilerParams(vmem_limit_bytes=VMEM),
        cost_estimate=cost(1024, steps * DEPTH, 1024 * WIDE * 4),
        name="rest_products",
    )(place, *blocks, *weights)


def main_kernel(count, place_ref, *refs):
    x_refs, w_refs, tag_refs = refs[:count], refs[count : count + 5], refs[count + 5 : 2 * count + 5]
    before_ref, base_ref, moment_ref, sketch_ref, total = refs[2 * count + 5 :]
    step = pl.program_id(0)
    parts = products(x_refs, w_refs)
    rows = total.shape[0]
    places = [slice(i * FF, i * FF + part.shape[1]) for i, part in enumerate(parts)]

    @pl.when(step == 0)
    def _():
        for lanes, part in zip(places, parts):
            total[:, lanes] = before_ref[:, :, :, :, lanes].reshape(rows, part.shape[1]) + part

    @pl.when(step > 0)
    def _():
        for lanes, part in zip(places, parts):
            total[:, lanes] += part

    @pl.when(step == MAIN - 1)
    def _():
        tag = jnp.concatenate([r[...].astype(jnp.float32) for r in tag_refs], axis=0)
        lane = lax.broadcasted_iota(jnp.int32, tag.shape, 1)
        mask = jnp.sum(jnp.where(lane == place_ref[0], tag, 0.0), axis=1, keepdims=True)
        wide = total[:, places[4]].astype(jnp.bfloat16).astype(jnp.float32)
        zeros = jnp.zeros((rows, ROWS_OUT - SKETCH - 1), jnp.float32)
        left = jnp.concatenate([wide * mask, mask, zeros], axis=1).astype(jnp.bfloat16)
        for i in range(2):
            gate = total[:, places[i]]
            hidden = (gate / (1.0 + jnp.exp(-gate)) * total[:, places[2 + i]]).astype(jnp.bfloat16)
            moment_ref[:, places[i]] = base_ref[:, places[i]] + lax.dot_general(
                left, hidden, CONTRACT, preferred_element_type=jnp.float32
            )
        counts = tag[:, EXPERTS : EXPERTS + SKETCH]
        sketch_ref[...] = jnp.concatenate([wide, counts], axis=1).reshape(sketch_ref.shape)


def main_products(place, blocks, weights, before, base):
    count = len(blocks)
    rows = sum(b.shape[0] for b in blocks)
    last = MAIN * DEPTH // LANES
    return pl.pallas_call(
        functools.partial(main_kernel, count),
        grid_spec=pltpu.PrefetchScalarGridSpec(
            num_scalar_prefetch=1,
            grid=(MAIN,),
            in_specs=[pl.BlockSpec((b.shape[0], DEPTH), lambda k, e: (0, k)) for b in blocks]
            + weight_specs(weights, 0)
            + [pl.BlockSpec((b.shape[0], LANES), lambda k, e: (0, last)) for b in blocks]
            + [
                pl.BlockSpec(before.shape, lambda k, e: (0, 0, 0, 0, 0)),
                pl.BlockSpec(base.shape, lambda k, e: (0, 0)),
            ],
            out_specs=[
                pl.BlockSpec(base.shape, lambda k, e: (0, 0)),
                pl.BlockSpec((*before.shape[:4], LANES), lambda k, e: (0, 0, 0, 0, 0)),
            ],
            scratch_shapes=[pltpu.VMEM((rows, WIDE), jnp.float32)],
        ),
        out_shape=[
            jax.ShapeDtypeStruct(base.shape, jnp.float32),
            jax.ShapeDtypeStruct((*before.shape[:4], LANES), jnp.float32),
        ],
        compiler_params=pltpu.CompilerParams(vmem_limit_bytes=VMEM),
        cost_estimate=cost(rows, MAIN * DEPTH, rows * WIDE * 4),
        name="main_products",
    )(place, *blocks, *weights, *blocks, before, base)


def gram_kernel(place_ref, near_ref, far_ref, out_ref, all_ref):
    for ref, at, v in ((near_ref, 0, 0), (near_ref, 1, 1), (near_ref, 2, 3), (far_ref, 0, 2)):
        for u in range(4):
            for z in range(8):
                all_ref[
                    lax.rem(place_ref[3] + v, 4), lax.rem(place_ref[4] + u, 4), lax.rem(place_ref[5] + z, 8)
                ] = ref[at, u, z]
    whole = all_ref[...].reshape(-1, LANES)
    wide = whole[:, :SKETCH]
    sketch = wide.astype(jnp.bfloat16)
    for g in range(GROUPS):
        scaled = wide * whole[:, SKETCH + g : SKETCH + g + 1]
        high = scaled.astype(jnp.bfloat16)
        low = (scaled - high.astype(jnp.float32)).astype(jnp.bfloat16)
        both = lax.dot_general(sketch, high, CONTRACT, preferred_element_type=jnp.float32)
        out_ref[g] = both + lax.dot_general(sketch, low, CONTRACT, preferred_element_type=jnp.float32)


def gram_of(place, near, far):
    whole = pl.BlockSpec(memory_space=pltpu.VMEM)
    return pl.pallas_call(
        gram_kernel,
        in_specs=[pl.BlockSpec(memory_space=pltpu.SMEM), whole, whole],
        out_specs=whole,
        out_shape=jax.ShapeDtypeStruct((GROUPS, SKETCH, SKETCH), jnp.float32),
        scratch_shapes=[pltpu.VMEM((4, 4, 8, 8, LANES), jnp.float32)],
        name="gram",
    )(place, near, far)


def down_kernel(place_ref, own_ref, other_ref, w0_ref, w1_ref, out_ref):
    width = w0_ref.shape[0]
    total = None
    for left, weight in (
        (own_ref[:, :width] + other_ref[:, width:], w0_ref),
        (own_ref[:, width:] + other_ref[:, :width], w1_ref),
    ):
        high = left.astype(jnp.bfloat16)
        low = (left - high.astype(jnp.float32)).astype(jnp.bfloat16)
        both = jnp.dot(high, weight[...], preferred_element_type=jnp.float32)
        both += jnp.dot(low, weight[...], preferred_element_type=jnp.float32)
        total = both if total is None else total + both
    for t in range(out_ref.shape[1]):
        out_ref[0, t] = total[:, t * LANES : (t + 1) * LANES].astype(out_ref.dtype)


def down_moments(place, own, other, own_down, other_down, blocks):
    ff, columns = own_down.shape
    block = columns // (2 * blocks)
    left = pl.BlockSpec((ROWS_OUT, 2 * ff), lambda j, p: (0, 0))
    weight = pl.BlockSpec((ff, block), lambda j, p: (0, 2 * j + p[2]))
    return pl.pallas_call(
        down_kernel,
        grid_spec=pltpu.PrefetchScalarGridSpec(
            num_scalar_prefetch=1,
            grid=(blocks,),
            in_specs=[left, left, weight, weight],
            out_specs=pl.BlockSpec((1, block // LANES, ROWS_OUT, LANES), lambda j, p: (j, 0, 0, 0)),
        ),
        out_shape=jax.ShapeDtypeStruct((blocks, block // LANES, ROWS_OUT, LANES), jnp.bfloat16),
        name="down_moments",
    )(place, own, other, own_down, other_down)


def shards(tokens, routes, group_of, sketch_map, gate_weight, up_weight, down_weight):
    gate, up, down = gate_weight[0], up_weight[0], down_weight[0]
    swap = functools.partial(lax.ppermute, axis_name="core", perm=[(0, 1), (1, 0)])
    at_y, core, at_x, at_z = (lax.axis_index(a) for a in AXES)
    n_y, n_xz = SIZES[0], SIZES[2] * SIZES[3]
    expert = at_x * SIZES[3] + at_z

    main, rest = tagged(group_of, routes, tokens)
    rest = straight(straight(rest, U, 4), V, 4)
    rest = ring_of_eight(rest, Z)
    main = straight(main, Z, 8)
    half = main.shape[0] // 2
    after, before = shift(main, U, 1), shift(main, U, -1)
    top = jnp.concatenate([main, after], axis=0)
    bottom = jnp.concatenate([shift(after[:half], U, 1), shift(before[half:], U, -1), before], axis=0)
    *near, far = ring_of_four(top, bottom, V)

    weights = (gate, swap(gate), up, swap(up), gathered_map(sketch_map, swap))
    other_down = swap(down)
    ff = down.shape[0]
    ring_v, ring_u = jnp.where(core == 0, at_y, at_x), jnp.where(core == 0, at_x, at_y)
    place = jnp.stack([expert, at_y, core, ring_v, ring_u, at_z])

    near_part, far_part = rest_products(place, rest, weights)
    nothing = jnp.zeros((ROWS_OUT, 2 * ff), jnp.float32)
    near = [half for block in near for half in block]
    own, near_sketch = main_products(place, near, weights, near_part, nothing)
    own, far_sketch = main_products(place, far, weights, far_part, own)
    other = swap(own)
    gram = gram_of(place, near_sketch, far_sketch)
    factor = 1.0 / math.sqrt(4 * 8 * n_xz)
    gram_moment = (gram + swap(gram)) * (factor * factor)

    parts = down_moments(place, own, other, down, other_down, n_y)
    parts = lax.all_to_all(parts, "y", split_axis=0, concat_axis=0, tiled=True)
    block = jnp.sum(parts.astype(jnp.float32), axis=0)
    tiles = block.shape[0]
    block = block.reshape(tiles * ROWS_OUT, LANES)
    share = -(-block.shape[0] // (8 * n_xz)) * 8
    block = jnp.pad(block, ((0, share * n_xz - block.shape[0]), (0, 0)))
    pieces = lax.all_to_all(
        block.reshape(n_xz, share, LANES), ("x", "z"), split_axis=0, concat_axis=0, tiled=True
    )
    member = (group_of[:, None] == lax.iota(jnp.int32, GROUPS)[None, :]).astype(jnp.float32)
    summed = jnp.einsum("eg,erl->grl", member, pieces, precision=lax.Precision.HIGHEST) * factor
    summed = summed.astype(jnp.bfloat16)
    spread = jnp.broadcast_to(summed[None], (n_xz, *summed.shape))
    spread = lax.all_to_all(spread, ("x", "z"), split_axis=0, concat_axis=0, tiled=True)
    whole = spread.transpose(1, 0, 2, 3).reshape(GROUPS, n_xz * share, LANES)
    whole = whole[:, : tiles * ROWS_OUT].reshape(GROUPS, tiles, ROWS_OUT, LANES)
    whole = whole.astype(jnp.float32).transpose(0, 2, 1, 3).reshape(GROUPS, ROWS_OUT, tiles * LANES)
    return whole[:, :SKETCH], gram_moment, whole[:, SKETCH]


def solution(mesh):
    fine = Mesh(mesh.devices.reshape(SIZES), AXES)
    dp, expert = ("y", "core"), ("x", "z")
    placed = (
        P((*dp, *expert), None),
        P((*dp, *expert), None),
        P(),
        P(dp, None),
        P(expert, None, dp),
        P(expert, None, dp),
        P(expert, dp, None),
    )
    return jax.shard_map(
        shards,
        mesh=fine,
        in_specs=placed,
        out_specs=(P(None, None, dp), P(), P(None, dp)),
        check_vma=False,
    )
```

```python
import functools
import itertools
import math

import jax
import jax.numpy as jnp
from jax import lax
from jax.experimental import pallas as pl
from jax.experimental.pallas import tpu as pltpu
from jax.sharding import Mesh
from jax.sharding import PartitionSpec as P

EXPERTS = 32
GROUPS = 8
SKETCH = 64
LANES = 128
ROWS_OUT = 72
DEPTH = 896
MAIN = 6
AXES = ("y", "core", "x", "z")
SIZES = (4, 2, 4, 8)
U, V, Z = ("x", "y"), ("y", "x"), ("z", "z")
FF = 256
WIDE = 4 * FF + LANES
VMEM = 48 * 2**20
CONTRACT = (((0,), (0,)), ((), ()))


def shift(block, ring, places):
    pairs = []
    for at in itertools.product(*(range(n) for n in SIZES)):
        source = list(at)
        axis = AXES.index(ring[at[1]])
        source[axis] = (source[axis] + places) % SIZES[axis]
        number = [0, 0]
        for n, a, b in zip(SIZES, source, at):
            number = [number[0] * n + a, number[1] * n + b]
        pairs.append(tuple(number))
    return lax.ppermute(block, AXES, pairs)


def straight(block, ring, size):
    return jnp.concatenate([block] + [shift(block, ring, k) for k in range(1, size)], axis=0)


def ring_of_four(top, bottom, ring):
    after = (shift(top, ring, 1), shift(bottom, ring, 1))
    before = (shift(top, ring, -1), shift(bottom, ring, -1))
    far = (shift(after[0], ring, 1), shift(before[1], ring, -1))
    return (top, bottom), after, before, far


def ring_of_eight(block, ring):
    half = block.shape[0] // 2
    after, before = [shift(block, ring, 1)], [shift(block, ring, -1)]
    for _ in range(2):
        after.append(shift(after[-1], ring, 1))
        before.append(shift(before[-1], ring, -1))
    far = [shift(after[-1][:half], ring, 1), shift(before[-1][half:], ring, -1)]
    return [block, *after, *far, *before[::-1]]


def tag_kernel(group_ref, routes_ref, tokens_ref, main_ref, rest_ref):
    routes = routes_ref[...]
    group = jnp.zeros(routes.shape, jnp.int32)
    for e in range(EXPERTS):
        group = jnp.where(routes == e, group_ref[e], group)
    lane = lax.broadcasted_iota(jnp.int32, (routes.shape[0], LANES), 1)
    tag = jnp.zeros(lane.shape, jnp.float32)
    for j in range(routes.shape[1]):
        tag += jnp.where(lane == routes[:, j : j + 1], 1.0, 0.0)
        tag += jnp.where(lane == EXPERTS + group[:, j : j + 1], 1.0, 0.0)
    split = rest_ref.shape[1]
    main_ref[:, : MAIN * DEPTH] = tokens_ref[:, : MAIN * DEPTH]
    main_ref[:, MAIN * DEPTH :] = tag.astype(jnp.bfloat16)
    rest_ref[...] = tokens_ref[:, tokens_ref.shape[1] - split :]


def tagged(group_of, routes, tokens):
    rows, width = tokens.shape
    whole = pl.BlockSpec(memory_space=pltpu.VMEM)
    return pl.pallas_call(
        tag_kernel,
        in_specs=[pl.BlockSpec(memory_space=pltpu.SMEM), whole, whole],
        out_specs=[whole, whole],
        out_shape=[
            jax.ShapeDtypeStruct((rows, MAIN * DEPTH + LANES), tokens.dtype),
            jax.ShapeDtypeStruct((rows, width - MAIN * DEPTH), tokens.dtype),
        ],
        name="tag",
    )(group_of, routes, tokens)


def gathered_map(sketch_map, swap):
    half = sketch_map.shape[0] // 2
    own = jnp.concatenate([sketch_map[:half], sketch_map[half:]], axis=1)
    return straight(jnp.stack([own, swap(own)]), ("y", "y"), 4)


def map_block(k, place_ref):
    return lax.rem(k // 2 + 4 - place_ref[1], 4) * 2 + lax.rem(k + place_ref[2], 2), 0, 0


def products(x_refs, w_refs):
    x = jnp.concatenate([r[...] for r in x_refs], axis=0) if len(x_refs) > 1 else x_refs[0][...]
    sides = w_refs[4][0]
    weights = [r[...] for r in w_refs[:4]]
    weights.append(jnp.concatenate([sides[:, :SKETCH], sides[:, SKETCH:]], axis=0))
    return [jnp.dot(x, w, preferred_element_type=jnp.float32) for w in weights]


def weight_specs(weights, first):
    half = weights[4].shape[1]
    return [pl.BlockSpec((DEPTH, w.shape[1]), lambda k, p: (first + k, 0)) for w in weights[:4]] + [
        pl.BlockSpec((1, half, LANES), lambda k, p: map_block(first + k, p))
    ]


def rest_kernel(count, place_ref, *refs):
    x_refs, w_refs, (near_ref, far_ref) = refs[:count], refs[count:-2], refs[-2:]
    step = pl.program_id(0)
    parts = products(x_refs, w_refs)

    def put(ref, at, z, lanes, value):
        @pl.when(step == 0)
        def _():
            ref[at, :, z, :, lanes] = value

        @pl.when(step > 0)
        def _():
            ref[at, :, z, :, lanes] += value

    for i, part in enumerate(parts):
        lanes = slice(i * FF, i * FF + part.shape[1])
        part = part.reshape(8, 4, 4, 8, part.shape[1])
        for z in range(8):
            for at, v in enumerate((0, 1, 3)):
                put(near_ref, at, z, lanes, part[z, v])
            put(far_ref, 0, z, lanes, part[z, 2])


def cost(rows, depth, out_bytes):
    return pl.CostEstimate(
        flops=2 * rows * depth * 5 * FF, bytes_accessed=depth * (rows + WIDE) * 2 + out_bytes, transcendentals=0
    )


def rest_products(place, blocks, weights):
    steps = blocks[0].shape[1] // DEPTH
    shape = (4, 8, 8, WIDE)
    return pl.pallas_call(
        functools.partial(rest_kernel, len(blocks)),
        grid_spec=pltpu.PrefetchScalarGridSpec(
            num_scalar_prefetch=1,
            grid=(steps,),
            in_specs=[pl.BlockSpec((b.shape[0], DEPTH), lambda k, p: (0, k)) for b in blocks]
            + weight_specs(weights, MAIN),
            out_specs=[pl.BlockSpec((n, *shape), lambda k, p: (0, 0, 0, 0, 0)) for n in (3, 1)],
        ),
        out_shape=[jax.ShapeDtypeStruct((n, *shape), jnp.float32) for n in (3, 1)],
        compiler_params=pltpu.CompilerParams(vmem_limit_bytes=VMEM),
        cost_estimate=cost(1024, steps * DEPTH, 1024 * WIDE * 4),
        name="rest_products",
    )(place, *blocks, *weights)


def main_kernel(count, place_ref, *refs):
    x_refs, w_refs, tag_refs = refs[:count], refs[count : count + 5], refs[count + 5 : 2 * count + 5]
    before_ref, base_ref, moment_ref, sketch_ref, total = refs[2 * count + 5 :]
    step = pl.program_id(0)
    parts = products(x_refs, w_refs)
    rows = total.shape[0]
    places = [slice(i * FF, i * FF + part.shape[1]) for i, part in enumerate(parts)]

    @pl.when(step == 0)
    def _():
        for lanes, part in zip(places, parts):
            total[:, lanes] = before_ref[:, :, :, :, lanes].reshape(rows, part.shape[1]) + part

    @pl.when(step > 0)
    def _():
        for lanes, part in zip(places, parts):
            total[:, lanes] += part

    @pl.when(step == MAIN - 1)
    def _():
        tag = jnp.concatenate([r[...].astype(jnp.float32) for r in tag_refs], axis=0)
        lane = lax.broadcasted_iota(jnp.int32, tag.shape, 1)
        mask = jnp.sum(jnp.where(lane == place_ref[0], tag, 0.0), axis=1, keepdims=True)
        wide = total[:, places[4]].astype(jnp.bfloat16).astype(jnp.float32)
        zeros = jnp.zeros((rows, ROWS_OUT - SKETCH - 1), jnp.float32)
        left = jnp.concatenate([wide * mask, mask, zeros], axis=1).astype(jnp.bfloat16)
        for i in range(2):
            gate = total[:, places[i]]
            hidden = (gate / (1.0 + jnp.exp(-gate)) * total[:, places[2 + i]]).astype(jnp.bfloat16)
            moment_ref[:, places[i]] = base_ref[:, places[i]] + lax.dot_general(
                left, hidden, CONTRACT, preferred_element_type=jnp.float32
            )
        counts = tag[:, EXPERTS : EXPERTS + SKETCH]
        sketch_ref[...] = jnp.concatenate([wide, counts], axis=1).reshape(sketch_ref.shape)


def main_products(place, blocks, weights, before, base):
    count = len(blocks)
    rows = sum(b.shape[0] for b in blocks)
    last = MAIN * DEPTH // LANES
    return pl.pallas_call(
        functools.partial(main_kernel, count),
        grid_spec=pltpu.PrefetchScalarGridSpec(
            num_scalar_prefetch=1,
            grid=(MAIN,),
            in_specs=[pl.BlockSpec((b.shape[0], DEPTH), lambda k, e: (0, k)) for b in blocks]
            + weight_specs(weights, 0)
            + [pl.BlockSpec((b.shape[0], LANES), lambda k, e: (0, last)) for b in blocks]
            + [
                pl.BlockSpec(before.shape, lambda k, e: (0, 0, 0, 0, 0)),
                pl.BlockSpec(base.shape, lambda k, e: (0, 0)),
            ],
            out_specs=[
                pl.BlockSpec(base.shape, lambda k, e: (0, 0)),
                pl.BlockSpec((*before.shape[:4], LANES), lambda k, e: (0, 0, 0, 0, 0)),
            ],
            scratch_shapes=[pltpu.VMEM((rows, WIDE), jnp.float32)],
        ),
        out_shape=[
            jax.ShapeDtypeStruct(base.shape, jnp.float32),
            jax.ShapeDtypeStruct((*before.shape[:4], LANES), jnp.float32),
        ],
        compiler_params=pltpu.CompilerParams(vmem_limit_bytes=VMEM),
        cost_estimate=cost(rows, MAIN * DEPTH, rows * WIDE * 4),
        name="main_products",
    )(place, *blocks, *weights, *blocks, before, base)


def gram_kernel(place_ref, near_ref, far_ref, out_ref, all_ref):
    for ref, at, v in ((near_ref, 0, 0), (near_ref, 1, 1), (near_ref, 2, 3), (far_ref, 0, 2)):
        for u in range(4):
            for z in range(8):
                all_ref[
                    lax.rem(place_ref[3] + v, 4), lax.rem(place_ref[4] + u, 4), lax.rem(place_ref[5] + z, 8)
                ] = ref[at, u, z]
    whole = all_ref[...].reshape(-1, LANES)
    wide = whole[:, :SKETCH]
    sketch = wide.astype(jnp.bfloat16)
    for g in range(GROUPS):
        scaled = wide * whole[:, SKETCH + g : SKETCH + g + 1]
        high = scaled.astype(jnp.bfloat16)
        low = (scaled - high.astype(jnp.float32)).astype(jnp.bfloat16)
        both = lax.dot_general(sketch, high, CONTRACT, preferred_element_type=jnp.float32)
        out_ref[g] = both + lax.dot_general(sketch, low, CONTRACT, preferred_element_type=jnp.float32)


def gram_of(place, near, far):
    whole = pl.BlockSpec(memory_space=pltpu.VMEM)
    return pl.pallas_call(
        gram_kernel,
        in_specs=[pl.BlockSpec(memory_space=pltpu.SMEM), whole, whole],
        out_specs=whole,
        out_shape=jax.ShapeDtypeStruct((GROUPS, SKETCH, SKETCH), jnp.float32),
        scratch_shapes=[pltpu.VMEM((4, 4, 8, 8, LANES), jnp.float32)],
        name="gram",
    )(place, near, far)


def down_kernel(place_ref, own_ref, other_ref, w0_ref, w1_ref, out_ref):
    width = w0_ref.shape[0]
    total = None
    for left, weight in (
        (own_ref[:, :width] + other_ref[:, width:], w0_ref),
        (own_ref[:, width:] + other_ref[:, :width], w1_ref),
    ):
        high = left.astype(jnp.bfloat16)
        low = (left - high.astype(jnp.float32)).astype(jnp.bfloat16)
        both = jnp.dot(high, weight[...], preferred_element_type=jnp.float32)
        both += jnp.dot(low, weight[...], preferred_element_type=jnp.float32)
        total = both if total is None else total + both
    for t in range(out_ref.shape[1]):
        out_ref[0, t] = total[:, t * LANES : (t + 1) * LANES].astype(out_ref.dtype)


def down_moments(place, own, other, own_down, other_down, blocks):
    ff, columns = own_down.shape
    block = columns // (2 * blocks)
    left = pl.BlockSpec((ROWS_OUT, 2 * ff), lambda j, p: (0, 0))
    weight = pl.BlockSpec((ff, block), lambda j, p: (0, 2 * lax.rem(p[1] + j, blocks) + p[2]))
    return pl.pallas_call(
        down_kernel,
        grid_spec=pltpu.PrefetchScalarGridSpec(
            num_scalar_prefetch=1,
            grid=(blocks,),
            in_specs=[left, left, weight, weight],
            out_specs=pl.BlockSpec((1, block // LANES, ROWS_OUT, LANES), lambda j, p: (j, 0, 0, 0)),
        ),
        out_shape=jax.ShapeDtypeStruct((blocks, block // LANES, ROWS_OUT, LANES), jnp.bfloat16),
        name="down_moments",
    )(place, own, other, own_down, other_down)


def shards(tokens, routes, group_of, sketch_map, gate_weight, up_weight, down_weight):
    gate, up, down = gate_weight[0], up_weight[0], down_weight[0]
    swap = functools.partial(lax.ppermute, axis_name="core", perm=[(0, 1), (1, 0)])
    at_y, core, at_x, at_z = (lax.axis_index(a) for a in AXES)
    n_y, n_xz = SIZES[0], SIZES[2] * SIZES[3]
    expert = at_x * SIZES[3] + at_z

    main, rest = tagged(group_of, routes, tokens)
    rest = straight(straight(rest, U, 4), V, 4)
    rest = ring_of_eight(rest, Z)
    main = straight(main, Z, 8)
    half = main.shape[0] // 2
    after, before = shift(main, U, 1), shift(main, U, -1)
    top = jnp.concatenate([main, after], axis=0)
    bottom = jnp.concatenate([shift(after[:half], U, 1), shift(before[half:], U, -1), before], axis=0)
    *near, far = ring_of_four(top, bottom, V)

    weights = (gate, swap(gate), up, swap(up), gathered_map(sketch_map, swap))
    other_down = swap(down)
    ff = down.shape[0]
    ring_v, ring_u = jnp.where(core == 0, at_y, at_x), jnp.where(core == 0, at_x, at_y)
    place = jnp.stack([expert, at_y, core, ring_v, ring_u, at_z])

    near_part, far_part = rest_products(place, rest, weights)
    nothing = jnp.zeros((ROWS_OUT, 2 * ff), jnp.float32)
    near = [half for block in near for half in block]
    own, near_sketch = main_products(place, near, weights, near_part, nothing)
    own, far_sketch = main_products(place, far, weights, far_part, own)
    other = swap(own)
    gram = gram_of(place, near_sketch, far_sketch)
    factor = 1.0 / math.sqrt(4 * 8 * n_xz)
    gram_moment = (gram + swap(gram)) * (factor * factor)

    parts = down_moments(place, own, other, down, other_down, n_y)
    parts = [parts[0]] + [shift(parts[k], ("y", "y"), -k) for k in range(1, n_y)]
    block = sum(part.astype(jnp.float32) for part in parts)
    tiles = block.shape[0]
    block = block.reshape(tiles * ROWS_OUT, LANES)
    share = -(-block.shape[0] // (8 * n_xz)) * 8
    block = jnp.pad(block, ((0, share * n_xz - block.shape[0]), (0, 0)))
    pieces = lax.all_to_all(
        block.reshape(n_xz, share, LANES), ("x", "z"), split_axis=0, concat_axis=0, tiled=True
    )
    member = (group_of[:, None] == lax.iota(jnp.int32, GROUPS)[None, :]).astype(jnp.float32)
    summed = jnp.einsum("eg,erl->grl", member, pieces, precision=lax.Precision.HIGHEST) * factor
    summed = summed.astype(jnp.bfloat16)
    spread = jnp.broadcast_to(summed[None], (n_xz, *summed.shape))
    spread = lax.all_to_all(spread, ("x", "z"), split_axis=0, concat_axis=0, tiled=True)
    whole = spread.transpose(1, 0, 2, 3).reshape(GROUPS, n_xz * share, LANES)
    whole = whole[:, : tiles * ROWS_OUT].reshape(GROUPS, tiles, ROWS_OUT, LANES)
    whole = whole.astype(jnp.float32).transpose(0, 2, 1, 3).reshape(GROUPS, ROWS_OUT, tiles * LANES)
    return whole[:, :SKETCH], gram_moment, whole[:, SKETCH]


def solution(mesh):
    fine = Mesh(mesh.devices.reshape(SIZES), AXES)
    dp, expert = ("y", "core"), ("x", "z")
    placed = (
        P((*dp, *expert), None),
        P((*dp, *expert), None),
        P(),
        P(dp, None),
        P(expert, None, dp),
        P(expert, None, dp),
        P(expert, dp, None),
    )
    return jax.shard_map(
        shards,
        mesh=fine,
        in_specs=placed,
        out_specs=(P(None, None, dp), P(), P(None, dp)),
        check_vma=False,
    )
```
